512 devices in a mesh: scen: 128 (over y, z_lo, x), dec: 4 (over z_hi, core).
Axes of the slice: x: 4, y: 4, z: 16 (z_hi: 2, z_lo: 8; z = z_hi * 8 + z_lo), core: 2. Of those that a mesh axis runs over, the one named last changes fastest.
Arguments:
- scen_duals: bfloat16 [32768, 1536], P('scen'), may hold values from -4.5 to 4.5
- recourse: bfloat16 [4, 1536, 4096], P(None, 'scen', 'dec'), may hold values from -0.15625 to 0.15625
- tile_active: int32 [32768, 12], P('scen'), may hold values 0 or 1
- scen_weights: float32 [32768], P('scen'), may hold values from 0.25 to 4
- cut_table: bfloat16 [2048, 8, 4096], P('scen', None, 'dec'), may hold values from -6 to 6
- cut_count: int32 [2048], P('scen'), may hold values from 0 to 7
- center: float32 [2048, 4096], P('scen', 'dec'), may hold values from -6 to 6
Outputs:
- node_means: float32 [4, 2048, 4096], P(None, 'scen', 'dec')
- new_cuts: bfloat16 [2048, 8, 4096], P('scen', None, 'dec')
- new_center: float32 [2048, 4096], P('scen', 'dec')
- scen_subgrads: bfloat16 [4, 32768, 4096], P(None, 'scen', 'dec')
The draws below stay inside these ranges and needn't reach their ends.
All inputs are finite; a program needn't handle non-finite values. No bound on the sum of `tile_active` on one device may be relied on, other than what follows from the above.
Results may differ from the reference program's by a relative error of at most 0.001.
Values may be sent and summed in bfloat16 or wider, within the bound.
No kernel may reach another device: no remote copies, remote signals or barrier semaphores. Data moves between devices by JAX's collectives and lax.ppermute only.
A program may use at most 128 MiB of HBM per device.

```python
import math
import jax
import jax.numpy as jnp
from jax import lax

D = 4096
M = 1536
SECTIONS = 4
LEAF = 16
CUTS = 8
SCEN = 32768
NB = 2048
MB = 12


def draw_scen_duals(key, part):
    key = jax.random.fold_in(key, 11)
    common = jnp.clip(jax.random.normal(jax.random.fold_in(key, 1), (M,), jnp.float32), -3.0, 3.0)
    rough = jnp.clip(jax.random.normal(jax.random.fold_in(key, 3), (SCEN, M), jnp.float32), -3.0, 3.0)
    return (common[None, :] + 0.5 * rough).astype(jnp.bfloat16)


def touch_ends(entries, key, smallest, top_value):
    spot = [jax.random.randint(jax.random.fold_in(key, axis), (), 0, length) for axis, length in enumerate(entries.shape)]
    main_axis = entries.shape.index(max(entries.shape))
    neighbour = spot[:main_axis] + [(spot[main_axis] + 1) % entries.shape[main_axis]] + spot[main_axis + 1:]
    return entries.at[tuple(spot)].set(smallest).at[tuple(neighbour)].set(top_value)


def levels(own_key, extent, shards, low, high):
    def one(axis_at, blocks):
        steps = jax.random.uniform(jax.random.fold_in(jax.random.fold_in(own_key, 6), axis_at), (blocks,), jnp.float32, low / len(shards), high / len(shards))
        return jnp.repeat(jnp.exp(steps), extent[axis_at] // blocks).reshape((-1,) + (1,) * (len(extent) - axis_at - 1))

    loudness = one(*shards[0])
    for cut in shards[1:]:
        loudness = loudness * one(*cut)
    return loudness


def normal_values(stream_key, extent, width, reach, pieces=(), held_as=jnp.bfloat16):
    entries = jax.random.normal(stream_key, extent, jnp.float32) * width
    if len(pieces) > 0:
        entries = levels(stream_key, extent, pieces, -0.22, 0.18) * entries
    return jnp.clip(entries, min=-reach, max=reach).astype(held_as)


def setup_inputs(seed: int = 0) -> dict:
    seeds = jax.random.split(jax.random.key(seed), 8)
    return {
        "scen_duals": draw_scen_duals(jax.random.fold_in(seeds[7], 71), 0),
        "recourse": normal_values(seeds[1], (SECTIONS, M, D), M ** -0.5, 0.15625, ((1, 128), (2, 4))),
        "tile_active": touch_ends((jax.random.randint(seeds[2], (SCEN, MB), 0, 4) < 3).astype(jnp.int32), jax.random.fold_in(seeds[2], 1), 0, 1),
        "scen_weights": jnp.clip(jnp.exp(math.log(4.0) - 2.7725887 * jax.random.uniform(seeds[3], (SCEN,), jnp.float32) ** levels(seeds[3], (SCEN,), ((0, 128),), -0.2, 0.2)), 0.25, 4.0),
        "cut_table": normal_values(seeds[4], (NB, CUTS, D), 1.0, 6.0, ((0, 128), (2, 4))),
        "cut_count": touch_ends(jax.random.randint(seeds[5], (NB,), 0, CUTS), jax.random.fold_in(seeds[5], 1), 0, CUTS - 1).astype(jnp.int32),
        "center": normal_values(seeds[6], (NB, D), 1.0, 6.0, ((0, 128), (1, 4)), jnp.float32),
    }


step_size = 0.5

def reference(scen_duals, recourse, tile_active, scen_weights, cut_table, cut_count, center):
    scen_total, row_count = scen_duals.shape
    tile_count = tile_active.shape[1]
    masked = (scen_duals.reshape(scen_total, tile_count, row_count // tile_count) * tile_active.astype(scen_duals.dtype)[:, :, None]).reshape(scen_total, row_count)
    low_span = min(scen_total, LEAF * LEAF)
    mid_span = min(scen_total, LEAF * LEAF * LEAF)
    spans = [scen_total, mid_span, low_span, LEAF]
    section_means = []
    section_grads = []
    for section_num in range(SECTIONS):
        subgrad = jnp.dot(masked, recourse[section_num], preferred_element_type=jnp.float32)
        section_grads.append(subgrad.astype(jnp.bfloat16))
        weighted = subgrad * scen_weights[:, None]
        span_len = spans[section_num]
        node_sums = lax.optimization_barrier(jnp.sum(weighted.reshape(scen_total // span_len, span_len, D), axis=1))
        node_w = lax.optimization_barrier(jnp.sum(scen_weights.reshape(scen_total // span_len, span_len), axis=1))
        means_here = node_sums / node_w[:, None]
        section_means.append(jnp.repeat(means_here, span_len // LEAF, axis=0))
    node_means = jnp.stack(section_means)
    scen_subgrads = jnp.stack(section_grads)
    new_cut = node_means[SECTIONS - 1].astype(jnp.bfloat16)
    slot_ids = jnp.arange(CUTS, dtype=jnp.int32)
    slot_hit = slot_ids[None, :] == cut_count[:, None]
    new_cuts = jnp.where(slot_hit[:, :, None], new_cut[:, None, :], cut_table)
    active_slot = slot_ids[None, :] <= cut_count[:, None]
    summed_cuts = lax.optimization_barrier(jnp.sum(jnp.where(active_slot[:, :, None], new_cuts.astype(jnp.float32), 0.0), axis=1))
    aggregate = summed_cuts / (cut_count.astype(jnp.float32) + 1.0)[:, None]
    scale_rms = jnp.sqrt(lax.optimization_barrier(jnp.sum(aggregate * aggregate, axis=1)) / D + 1e-05)
    new_center = center - step_size * aggregate / scale_rms[:, None]
    return (node_means, new_cuts, new_center, scen_subgrads)
```

```python
import jax
import jax.numpy as jnp
from jax import lax
from jax.sharding import Mesh
from jax.sharding import PartitionSpec as P

LEAF = 16
STEP = 0.5
F32 = jnp.float32
BF16 = jnp.bfloat16

NY, NQ, NR, NX = 4, 2, 4, 4
SCEN = ("y", "zq", "zr", "x")
DEC = ("zh", "c")


def exchange(value, axes):
    return lax.all_to_all(value, axes, 0, 0, tiled=True)


def spread(value, axes, count):
    return exchange(jnp.broadcast_to(value[None], (count,) + value.shape), axes)


def split_two(value):
    high = lax.reduce_precision(value, 8, 7)
    return high.astype(BF16), (value - high).astype(BF16)


def local(scen_duals, recourse, tile_active, scen_weights, cut_table, cut_count, center):
    rows, depth = scen_duals.shape
    tiles = tile_active.shape[1]
    sections, own_rows, cols = recourse.shape
    half = cols // 2
    blocks = rows // LEAF

    first = jnp.broadcast_to(recourse[None, :, :, :half], (NQ, NX, own_rows, half))
    first = exchange(first.reshape(NQ * NX, own_rows, half), ("zq", "x"))
    second = jnp.broadcast_to(recourse[:, None, :, half:], (NY, NQ, own_rows, half))
    second = exchange(second.reshape(NY * NQ, own_rows, half), ("y", "zq"))
    first = first.reshape(NQ, NX * own_rows, half)
    second = jnp.swapaxes(second.reshape(NY, NQ, own_rows, half), 0, 1).reshape(NQ, NY * own_rows, half)
    both = spread(jnp.stack([first, second]), "zr", NR)
    both = jnp.transpose(both, (1, 2, 0, 3, 4))
    first = spread(both[0], "y", NY).reshape(depth, half)
    second = spread(both[1], "x", NX).reshape(depth, half)

    masked = (
        scen_duals.reshape(rows, tiles, depth // tiles) * tile_active.astype(BF16)[:, :, None]
    ).reshape(rows, depth)
    weighted = masked.astype(F32) * scen_weights[:, None]
    leaf_v = jnp.sum(weighted.reshape(blocks, LEAF, depth), axis=1)
    leaf_w = jnp.sum(scen_weights.reshape(blocks, LEAF), axis=1)
    own_v = jnp.sum(leaf_v, axis=0)
    own_w = jnp.sum(leaf_w)
    leaf_hi, leaf_lo = split_two(leaf_v / leaf_w[:, None])
    own_hi, own_lo = split_two((own_v / own_w)[None])
    sums = jnp.concatenate([leaf_hi, leaf_lo, own_hi, own_lo, jnp.zeros((14, depth), BF16)], 0)
    packed = jnp.concatenate([masked, sums], 0)
    order = jnp.arange(depth, dtype=jnp.int32).reshape(NY, NQ * NR, NX, own_rows)
    order = jnp.transpose(order, (2, 1, 0, 3)).reshape(depth)
    one_hot = (jnp.arange(depth, dtype=jnp.int32)[:, None] == order[None, :]).astype(BF16)
    packed_y = jnp.dot(packed, one_hot, preferred_element_type=F32).astype(BF16)
    duals_x = spread(packed, "x", NX)
    duals_y = spread(packed_y, "y", NY)

    tree = jnp.concatenate([own_v, own_w[None], jnp.zeros((511,), F32)]).reshape(16, 128)
    mid = jnp.sum(spread(tree, ("zr", "x"), NR * NX), axis=0)
    mids = spread(mid, ("y", "zq"), NY * NQ).reshape(NY, NQ, 2048)
    root = jnp.sum(mids, axis=(0, 1))[None]
    mine = lax.dynamic_index_in_dim(mids, lax.axis_index("zq"), 1, keepdims=False)
    upper = jnp.concatenate([mine, root], 0)
    upper = upper[:, :depth] / upper[:, depth][:, None]
    upper_hi, upper_lo = split_two(upper)
    upper_rows = jnp.concatenate([upper_hi, upper_lo, jnp.zeros((6, depth), BF16)], 0)
    upper_rows_y = jnp.dot(upper_rows, one_hot, preferred_element_type=F32).astype(BF16)

    def node_part(duals, tops, rhs, axis):
        left = jnp.concatenate([duals[:, rows:].reshape(4 * 48, depth), tops], 0)
        got = jnp.dot(left, rhs, preferred_element_type=F32)
        low = got[: 4 * 48].reshape(4, 48, half)
        leaves = low[:, :16] + low[:, 16:32]
        owns = low[:, 32:33] + low[:, 33:34]
        top = got[4 * 48 : 4 * 48 + 5] + got[4 * 48 + 5 : 4 * 48 + 10]
        if axis == "x":
            middle = lax.dynamic_slice_in_dim(top, lax.axis_index("y"), 1, 0)
            middle = jnp.broadcast_to(middle[None], (4, 1, half))
        else:
            middle = top[:4, None]
        base = jnp.broadcast_to(top[4][None, None], (4, 1, half))
        send = jnp.concatenate([leaves, owns, middle, base, jnp.zeros((4, 5, half), F32)], 1)
        return exchange(send, axis)

    def grad_part(duals, rhs, axis):
        left = duals[:, :rows].reshape(4 * rows, depth)
        got = jnp.dot(left, rhs, preferred_element_type=F32).astype(BF16)
        return exchange(got.reshape(4, rows, half), axis)

    nodes_x = node_part(duals_x, upper_rows, first, "x")
    nodes_y = node_part(duals_y, upper_rows_y, second, "y")
    grads_x = grad_part(duals_x, first, "x")
    grads_y = grad_part(duals_y, second, "y")
    scen_subgrads = jnp.concatenate([grads_x, grads_y], -1)

    nodes = jnp.concatenate([nodes_x, nodes_y], -1)
    leaf_means = nodes[3, :16]
    uppers = jnp.stack([nodes[0, 18], nodes[1, 17], nodes[2, 16]])
    node_means = jnp.concatenate(
        [jnp.broadcast_to(uppers[:, None, :], (3, blocks, cols)), leaf_means[None]], 0
    )

    new_cut = leaf_means.astype(BF16)
    slot_ids = jnp.arange(cut_table.shape[1], dtype=jnp.int32)
    slot_hit = slot_ids[None, :] == cut_count[:, None]
    new_cuts = jnp.where(slot_hit[:, :, None], new_cut[:, None, :], cut_table)
    active = slot_ids[None, :] <= cut_count[:, None]
    total = jnp.sum(jnp.where(active[:, :, None], new_cuts.astype(F32), 0.0), axis=1)
    aggregate = total / (cut_count.astype(F32) + 1.0)[:, None]
    squares = jnp.sum(aggregate * aggregate, axis=1)
    total_sq = lax.psum(squares, DEC)
    scale = jnp.sqrt(total_sq / (cols * 4) + 1e-05)
    new_center = center - STEP * aggregate / scale[:, None]
    return (node_means, new_cuts, new_center, scen_subgrads)


def solution(mesh):
    fine = Mesh(mesh.devices.reshape(NY, NQ, NR, NX, 2, 2), SCEN + DEC)
    placed = (
        P(SCEN, None),
        P(None, SCEN, DEC),
        P(SCEN, None),
        P(SCEN),
        P(SCEN, None, DEC),
        P(SCEN),
        P(SCEN, DEC),
    )
    return jax.shard_map(
        local,
        mesh=fine,
        in_specs=placed,
        out_specs=(
            P(None, SCEN, DEC),
            P(SCEN, None, DEC),
            P(SCEN, DEC),
            P(None, SCEN, DEC),
        ),
        check_vma=False,
    )
```

```python
import jax
import jax.numpy as jnp
from jax import lax
from jax.experimental import pallas as pl
from jax.experimental.pallas import tpu as pltpu
from jax.sharding import Mesh
from jax.sharding import PartitionSpec as P

LEAF = 16
STEP = 0.5
F32 = jnp.float32
BF16 = jnp.bfloat16
VMEM_LIMIT = 48 * 1024 * 1024

NY, NQ, NR, NX = 4, 2, 4, 4
NZ = NQ * NR
SCEN = ("y", "zq", "zr", "x")
DEC = ("zh", "c")
EXTRA = 48
ARRIVED = (0, 4, 2, 6, 1, 5, 3, 7)


def exchange(value, axes):
    return lax.all_to_all(value, axes, 0, 0, tiled=True)


def spread(value, axes, count):
    return exchange(jnp.broadcast_to(value[None], (count,) + value.shape), axes)


def shift(value, axis, count, step):
    return lax.ppermute(value, axis, [((i + step) % count, i) for i in range(count)])


def flip(value, distance):
    return lax.ppermute(value, ("zq", "zr"), [(i, i ^ distance) for i in range(NZ)])


def split_two(value):
    high = value.astype(BF16)
    return high, (value - high.astype(F32)).astype(BF16)


def params(**more):
    return pltpu.CompilerParams(vmem_limit_bytes=VMEM_LIMIT, **more)


def cost(flops, size):
    return pl.CostEstimate(flops=flops, bytes_accessed=size, transcendentals=0)


def prepare_body(duals_ref, active_ref, weight_ref, packed_ref, tree_ref):
    rows, depth = duals_ref.shape
    tiles = active_ref.shape[1]
    width = depth // tiles
    blocks = rows // LEAF
    weight = weight_ref[...]
    leaf_w = jnp.sum(weight.reshape(blocks, LEAF, 1), axis=1)
    own_w = jnp.sum(leaf_w, axis=0, keepdims=True)
    active = active_ref[...].astype(F32)

    def put(at_rows, at, value):
        packed_ref[at_rows, at] = value

    for tile in range(tiles):
        at = slice(tile * width, (tile + 1) * width)
        masked = duals_ref[:, at].astype(F32) * active[:, tile : tile + 1]
        put(slice(EXTRA, None), at, masked.astype(BF16))
        leaf_v = jnp.sum((masked * weight).reshape(blocks, LEAF, width), axis=1)
        own_v = jnp.sum(leaf_v, axis=0, keepdims=True)
        high, low = split_two(leaf_v / leaf_w)
        put(slice(0, 16), at, high)
        put(slice(16, 32), at, low)
        high, low = split_two(jnp.broadcast_to(own_v / own_w, (8, width)))
        put(slice(32, 48), at, jnp.concatenate([high, low], 0))
        tree_ref[:, at] = own_v
    tree_ref[:, depth:] = jnp.broadcast_to(own_w, (1, 128))


def prepare(duals, active, weights):
    rows, depth = duals.shape
    return pl.pallas_call(
        prepare_body,
        out_shape=(
            jax.ShapeDtypeStruct((rows + EXTRA, depth), BF16),
            jax.ShapeDtypeStruct((1, depth + 128), F32),
        ),
        compiler_params=params(),
        cost_estimate=cost(4 * rows * depth, 4 * rows * depth),
    )(duals, active, weights[:, None])


def products_body(x_ref, y_ref, z_ref, top_ref, left_ref, *refs):
    pieces, (nodes_ref, grads_ref, rhs_ref) = refs[:10], refs[10:]
    block = rhs_ref.shape[0] // (NY * NZ)

    def put(step, offset, value):
        place = lax.rem(y_ref[0] + step, NY) * NZ + (z_ref[0] ^ offset)
        rhs_ref[pl.ds(pl.multiple_of(place * block, block), block)] = value

    for part in range(2):
        here, up, down, over, under = pieces[5 * part : 5 * part + 5]
        for index, offset in enumerate(ARRIVED[4 * part : 4 * part + 4]):
            at = slice(index * block, (index + 1) * block)
            put(0, offset, here[at])
            put(1, offset, up[at])
            put(3, offset, down[at])
            put(2, offset, (over[at] if index < 2 else under[(index - 2) * block : (index - 1) * block]))
    rhs = rhs_ref[...]
    cols = rhs.shape[1]
    rows = left_ref.shape[0] // NX
    top = jnp.dot(top_ref[...], rhs, preferred_element_type=F32)
    middle = top[0:1] + top[1:2]
    base = top[2:3] + top[3:4]
    row = lax.broadcasted_iota(jnp.int32, (8, cols), 0)
    whole = jnp.dot(left_ref[...], rhs, preferred_element_type=F32)
    for to in range(NX):
        got = whole[to * rows : (to + 1) * rows]
        grads_ref[to] = got[EXTRA:].astype(BF16)
        step = lax.rem(to - x_ref[0] + NX, NX)
        nodes_ref[step, 0:16] = got[0:16] + got[16:32]
        mean = got[32:33] + got[40:41]
        nodes_ref[step, 16:24] = jnp.where(row == 0, mean, jnp.where(row == 1, middle, base))


def products(x_at, y_at, z_at, top, left, pieces):
    rows, depth = left.shape
    rows = rows // NX - EXTRA
    cols = pieces[0].shape[1]
    steps = 4
    wide = cols // steps
    whole = lambda value: pl.BlockSpec(value.shape, lambda j: (0, 0))
    return pl.pallas_call(
        products_body,
        grid=(steps,),
        in_specs=[pl.BlockSpec(memory_space=pltpu.SMEM)] * 3
        + [whole(top), whole(left)]
        + [pl.BlockSpec((value.shape[0], wide), lambda j: (0, j)) for value in pieces],
        out_specs=(
            pl.BlockSpec((NX, 24, wide), lambda j: (0, 0, j)),
            pl.BlockSpec((NX, rows, wide), lambda j: (0, 0, j)),
        ),
        out_shape=(
            jax.ShapeDtypeStruct((NX, 24, cols), F32),
            jax.ShapeDtypeStruct((NX, rows, cols), BF16),
        ),
        scratch_shapes=[pltpu.VMEM((depth, wide), BF16)],
        compiler_params=params(),
        cost_estimate=cost(2 * NX * (rows + EXTRA) * depth * cols, 10_000_000),
    )(x_at, y_at, z_at, top, left, *pieces)


def local(scen_duals, recourse, tile_active, scen_weights, cut_table, cut_count, center):
    rows, depth = scen_duals.shape
    sections, own_rows, cols = recourse.shape
    blocks = rows // LEAF
    x_at = lax.axis_index("x")[None]
    y_at = lax.axis_index("y")[None]
    z_at = lax.axis_index(("zq", "zr"))[None]
    together = lax.optimization_barrier

    own = exchange(recourse, "x").reshape(1, NX * own_rows, cols)
    packed, tree = prepare(scen_duals, tile_active, scen_weights)
    own, tree = together((own, tree))
    far = flip(own, 4)
    left = lax.all_gather(packed, "x", axis=0, tiled=True)
    pair = jnp.concatenate([own, far], 0)
    four = jnp.concatenate([pair, flip(pair, 2)], 0)
    late = flip(four, 1)
    middle = jnp.sum(spread(tree, ("zr", "x"), NR * NX), axis=0)
    base = jnp.sum(spread(middle, ("y", "zq"), NY * NQ), axis=0)

    four = four.reshape(-1, cols)
    late = late.reshape(-1, cols)
    half = four.shape[0] // 2
    four_up = shift(four, "y", NY, 1)
    four_down = shift(four, "y", NY, 3)
    late_up = shift(late, "y", NY, 1)
    late_down = shift(late, "y", NY, 3)
    four_over = shift(four_up[:half], "y", NY, 1)
    four_under = shift(four_down[half:], "y", NY, 3)
    late_over = shift(late_up[:half], "y", NY, 1)
    late_under = shift(late_down[half:], "y", NY, 3)
    pieces = (four, four_up, four_down, four_over, four_under)
    pieces += (late, late_up, late_down, late_over, late_under)

    upper = jnp.concatenate([middle, base], 0)
    upper = upper[:, :depth] / upper[:, depth : depth + 1]
    first = lax.reduce_precision(upper, 8, 7)
    second = (upper - first).astype(BF16)
    first = first.astype(BF16)
    top = jnp.concatenate([first[:1], second[:1], first[1:], second[1:], jnp.zeros((12, depth), BF16)], 0)

    nodes, grads = products(x_at, y_at, z_at, top, left, pieces)
    sent = [nodes[0]] + [shift(nodes[step], "x", NX, NX - step) for step in (1, 2, 3)]
    scen_subgrads = exchange(grads, "x")
    line = jnp.stack(sent)

    def of_section(section):
        return lax.dynamic_index_in_dim(line, lax.rem(x_at[0] - section + NX, NX), 0, keepdims=False)

    leaf_means = of_section(3)[:16]
    uppers = jnp.stack([of_section(0)[18], of_section(1)[17], of_section(2)[16]])
    node_means = jnp.concatenate(
        [jnp.broadcast_to(uppers[:, None, :], (3, blocks, cols)), leaf_means[None]], 0
    )
    new_cut = leaf_means.astype(BF16)
    slot_ids = jnp.arange(cut_table.shape[1], dtype=jnp.int32)
    slot_hit = slot_ids[None, :] == cut_count[:, None]
    new_cuts = jnp.where(slot_hit[:, :, None], new_cut[:, None, :], cut_table)
    active = slot_ids[None, :] <= cut_count[:, None]
    total = jnp.sum(jnp.where(active[:, :, None], new_cuts.astype(F32), 0.0), axis=1)
    aggregate = total / (cut_count.astype(F32) + 1.0)[:, None]
    squares = jnp.sum(aggregate * aggregate, axis=1)
    total_sq = lax.psum(squares, DEC)
    scale = jnp.sqrt(total_sq / (cols * 4) + 1e-05)
    new_center = center - STEP * aggregate / scale[:, None]
    return (node_means, new_cuts, new_center, scen_subgrads)


def solution(mesh):
    fine = Mesh(mesh.devices.reshape(NY, NQ, NR, NX, 2, 2), SCEN + DEC)
    placed = (
        P(SCEN, None),
        P(None, SCEN, DEC),
        P(SCEN, None),
        P(SCEN),
        P(SCEN, None, DEC),
        P(SCEN),
        P(SCEN, DEC),
    )
    return jax.shard_map(
        local,
        mesh=fine,
        in_specs=placed,
        out_specs=(
            P(None, SCEN, DEC),
            P(SCEN, None, DEC),
            P(SCEN, DEC),
            P(None, SCEN, DEC),
        ),
        check_vma=False,
    )
```

```python
import jax
import jax.numpy as jnp
from jax import lax
from jax.experimental import pallas as pl
from jax.experimental.pallas import tpu as pltpu
from jax.sharding import Mesh
from jax.sharding import PartitionSpec as P

LEAF = 16
STEP = 0.5
F32 = jnp.float32
BF16 = jnp.bfloat16
VMEM_LIMIT = 48 * 1024 * 1024

NY, NQ, NR, NX = 4, 2, 4, 4
NZ = NQ * NR
SCEN = ("y", "zq", "zr", "x")
DEC = ("zh", "c")
EXTRA = 48
ARRIVED = (0, 4, 2, 6, 1, 5, 3, 7)


def exchange(value, axes):
    return lax.all_to_all(value, axes, 0, 0, tiled=True)


def spread(value, axes, count):
    return exchange(jnp.broadcast_to(value[None], (count,) + value.shape), axes)


def shift(value, axis, count, step):
    return lax.ppermute(value, axis, [((i + step) % count, i) for i in range(count)])


def flip(value, distance):
    return lax.ppermute(value, ("zq", "zr"), [(i, i ^ distance) for i in range(NZ)])


def split_two(value):
    high = value.astype(BF16)
    return high, (value - high.astype(F32)).astype(BF16)


def params(**more):
    return pltpu.CompilerParams(vmem_limit_bytes=VMEM_LIMIT, **more)


def cost(flops, size):
    return pl.CostEstimate(flops=flops, bytes_accessed=size, transcendentals=0)


def prepare_body(duals_ref, active_ref, weight_ref, recourse_ref, packed_ref, send_ref):
    rows, depth = duals_ref.shape
    tiles = active_ref.shape[0]
    width = depth // tiles
    blocks = rows // LEAF
    cols = send_ref.shape[2]
    weight = jnp.transpose(jnp.broadcast_to(weight_ref[...], (8, rows)))[:, :1]
    leaf_w = jnp.sum(weight.reshape(blocks, LEAF, 1), axis=1)
    own_w = jnp.sum(leaf_w, axis=0, keepdims=True)
    active = jnp.transpose(active_ref[...].astype(F32))
    highs, lows = [], []
    for tile in range(tiles):
        at = slice(tile * width, (tile + 1) * width)
        masked = duals_ref[:, at].astype(F32) * active[:, tile : tile + 1]
        packed_ref[EXTRA:, at] = masked.astype(BF16)
        leaf_v = jnp.sum((masked * weight).reshape(blocks, LEAF, width), axis=1)
        own_v = jnp.sum(leaf_v, axis=0, keepdims=True)
        high, low = split_two(own_v)
        highs.append(high.astype(F32))
        lows.append(low.astype(F32))
        high, low = split_two(leaf_v / leaf_w)
        packed_ref[:16, at] = high
        packed_ref[16:32, at] = low
        high, low = split_two(jnp.broadcast_to(own_v / own_w, (8, width)))
        packed_ref[32:48, at] = jnp.concatenate([high, low], 0)
    high, low = jnp.concatenate(highs, 1), jnp.concatenate(lows, 1)
    w_high, w_low = split_two(jnp.broadcast_to(own_w, (1, cols // 2)))
    tree = jnp.concatenate(
        [
            high[:, :cols],
            low[:, :cols],
            jnp.concatenate([high[:, cols:], low[:, cols:]], 1),
            jnp.concatenate([w_high.astype(F32), w_low.astype(F32)], 1),
        ],
        0,
    )
    for section in range(NX):
        send_ref[section] = jnp.concatenate([recourse_ref[section].astype(F32), tree], 0).astype(BF16)


def prepare(duals, active, weights, recourse):
    rows, depth = duals.shape
    sections, own_rows, cols = recourse.shape
    return pl.pallas_call(
        prepare_body,
        out_shape=(
            jax.ShapeDtypeStruct((rows + EXTRA, depth), BF16),
            jax.ShapeDtypeStruct((NX, own_rows + 4, cols), BF16),
        ),
        compiler_params=params(),
        cost_estimate=cost(4 * rows * depth, 4 * rows * depth),
    )(duals, active.T, weights[None], recourse)


def unpack_body(got_ref, slot_ref, tree_ref):
    own_rows = got_ref.shape[1] - 4
    cols = got_ref.shape[2]
    extra = tree_ref.shape[1] - cols - 128
    got = [got_ref[x].astype(F32) for x in range(NX)]
    slot_ref[...] = jnp.concatenate([part[:own_rows] for part in got], 0).astype(BF16)
    tree = sum(part[own_rows:] for part in got)
    tree_ref[:, :cols] = tree[0:1] + tree[1:2]
    tree_ref[:, cols : cols + extra] = tree[2:3, :extra] + tree[2:3, extra:]
    tree_ref[:, cols + extra :] = tree[3:4, :128] + tree[3:4, cols // 2 : cols // 2 + 128]


def unpack(got, depth):
    _, rows, cols = got.shape
    return pl.pallas_call(
        unpack_body,
        out_shape=(
            jax.ShapeDtypeStruct((NX * (rows - 4), cols), BF16),
            jax.ShapeDtypeStruct((1, depth + 128), F32),
        ),
        compiler_params=params(),
        cost_estimate=cost(1000, 1000000),
    )(got)


def products_body(x_ref, y_ref, z_ref, top_ref, left_ref, *refs):
    pieces, (nodes_ref, grads_ref, rhs_ref) = refs[:10], refs[10:]
    block = rhs_ref.shape[0] // (NY * NZ)

    def put(step, offset, value):
        place = lax.rem(y_ref[0] + step, NY) * NZ + (z_ref[0] ^ offset)
        rhs_ref[pl.ds(pl.multiple_of(place * block, block), block)] = value

    for part in range(2):
        here, up, down, over, under = pieces[5 * part : 5 * part + 5]
        for index, offset in enumerate(ARRIVED[4 * part : 4 * part + 4]):
            at = slice(index * block, (index + 1) * block)
            put(0, offset, here[at])
            put(1, offset, up[at])
            put(3, offset, down[at])
            put(2, offset, (over[at] if index < 2 else under[(index - 2) * block : (index - 1) * block]))
    rhs = rhs_ref[...]
    cols = rhs.shape[1]
    rows = left_ref.shape[0] // NX
    top = jnp.dot(top_ref[...], rhs, preferred_element_type=F32)
    middle = top[0:1] + top[1:2]
    base = top[2:3] + top[3:4]
    row = lax.broadcasted_iota(jnp.int32, (8, cols), 0)
    whole = jnp.dot(left_ref[...], rhs, preferred_element_type=F32)
    for to in range(NX):
        got = whole[to * rows : (to + 1) * rows]
        grads_ref[to] = got[EXTRA:].astype(BF16)
        step = lax.rem(to - x_ref[0] + NX, NX)
        nodes_ref[step, 0:16] = got[0:16] + got[16:32]
        mean = got[32:33] + got[40:41]
        nodes_ref[step, 16:24] = jnp.where(row == 0, mean, jnp.where(row == 1, middle, base))


def products(x_at, y_at, z_at, top, left, pieces):
    rows, depth = left.shape
    rows = rows // NX - EXTRA
    cols = pieces[0].shape[1]
    steps = 2
    wide = cols // steps
    whole = lambda value: pl.BlockSpec(value.shape, lambda j: (0, 0))
    return pl.pallas_call(
        products_body,
        grid=(steps,),
        in_specs=[pl.BlockSpec(memory_space=pltpu.SMEM)] * 3
        + [whole(top), whole(left)]
        + [pl.BlockSpec((value.shape[0], wide), lambda j: (0, j)) for value in pieces],
        out_specs=(
            pl.BlockSpec((NX, 24, wide), lambda j: (0, 0, j)),
            pl.BlockSpec((NX, rows, wide), lambda j: (0, 0, j)),
        ),
        out_shape=(
            jax.ShapeDtypeStruct((NX, 24, cols), F32),
            jax.ShapeDtypeStruct((NX, rows, cols), BF16),
        ),
        scratch_shapes=[pltpu.VMEM((depth, wide), BF16)],
        compiler_params=params(),
        cost_estimate=cost(2 * NX * (rows + EXTRA) * depth * cols, 10_000_000),
    )(x_at, y_at, z_at, top, left, *pieces)


def local(scen_duals, recourse, tile_active, scen_weights, cut_table, cut_count, center):
    rows, depth = scen_duals.shape
    sections, own_rows, cols = recourse.shape
    blocks = rows // LEAF
    x_at = lax.axis_index("x")[None]
    y_at = lax.axis_index("y")[None]
    z_at = lax.axis_index(("zq", "zr"))[None]
    together = lax.optimization_barrier

    packed, send = prepare(scen_duals, tile_active, scen_weights, recourse)
    own, tree = unpack(exchange(send, "x"), depth)
    own = own[None]
    left = lax.all_gather(packed, "x", axis=0, tiled=True)
    far = flip(own, 4)
    pair = jnp.concatenate([own, far], 0)
    four = jnp.concatenate([pair, flip(pair, 2)], 0)
    late = flip(four, 1)
    row = jnp.sum(spread(tree, "y", NY), axis=0)
    trees = spread(jnp.concatenate([tree, row], 0), ("zq", "zr"), NZ)

    four = four.reshape(-1, cols)
    late = late.reshape(-1, cols)
    half = four.shape[0] // 2
    four_up = shift(four, "y", NY, 1)
    four_down = shift(four, "y", NY, 3)
    late_up = shift(late, "y", NY, 1)
    late_down = shift(late, "y", NY, 3)
    four_over = shift(four_up[:half], "y", NY, 1)
    four_under = shift(four_down[half:], "y", NY, 3)
    late_over = shift(late_up[:half], "y", NY, 1)
    late_under = shift(late_down[half:], "y", NY, 3)
    pieces = (four, four_up, four_down, four_over, four_under)
    pieces += (late, late_up, late_down, late_over, late_under)

    trees = jnp.sum(trees.reshape(NQ, NR, 2, depth + 128), axis=1)
    middle = lax.dynamic_index_in_dim(trees[:, 0], lax.axis_index("zq"), 0)
    base = jnp.sum(trees[:, 1], axis=0, keepdims=True)
    upper = jnp.concatenate([middle, base], 0)
    upper = upper[:, :depth] / upper[:, depth : depth + 1]
    first = lax.reduce_precision(upper, 8, 7)
    second = (upper - first).astype(BF16)
    first = first.astype(BF16)
    top = jnp.concatenate([first[:1], second[:1], first[1:], second[1:], jnp.zeros((12, depth), BF16)], 0)

    nodes, grads = products(x_at, y_at, z_at, top, left, pieces)
    sent = [nodes[0]] + [shift(nodes[step], "x", NX, NX - step) for step in (1, 2, 3)]
    scen_subgrads = exchange(grads, "x")
    line = jnp.stack(sent)

    def of_section(section):
        return lax.dynamic_index_in_dim(line, lax.rem(x_at[0] - section + NX, NX), 0, keepdims=False)

    leaf_means = of_section(3)[:16]
    uppers = jnp.stack([of_section(0)[18], of_section(1)[17], of_section(2)[16]])
    node_means = jnp.concatenate(
        [jnp.broadcast_to(uppers[:, None, :], (3, blocks, cols)), leaf_means[None]], 0
    )
    new_cut = leaf_means.astype(BF16)
    slot_ids = jnp.arange(cut_table.shape[1], dtype=jnp.int32)
    slot_hit = slot_ids[None, :] == cut_count[:, None]
    new_cuts = jnp.where(slot_hit[:, :, None], new_cut[:, None, :], cut_table)
    active = slot_ids[None, :] <= cut_count[:, None]
    total = jnp.sum(jnp.where(active[:, :, None], new_cuts.astype(F32), 0.0), axis=1)
    aggregate = total / (cut_count.astype(F32) + 1.0)[:, None]
    squares = jnp.sum(aggregate * aggregate, axis=1)
    total_sq = lax.psum(squares, DEC)
    scale = jnp.sqrt(total_sq / (cols * 4) + 1e-05)
    new_center = center - STEP * aggregate / scale[:, None]
    return (node_means, new_cuts, new_center, scen_subgrads)


def solution(mesh):
    fine = Mesh(mesh.devices.reshape(NY, NQ, NR, NX, 2, 2), SCEN + DEC)
    placed = (
        P(SCEN, None),
        P(None, SCEN, DEC),
        P(SCEN, None),
        P(SCEN),
        P(SCEN, None, DEC),
        P(SCEN),
        P(SCEN, DEC),
    )
    return jax.shard_map(
        local,
        mesh=fine,
        in_specs=placed,
        out_specs=(
            P(None, SCEN, DEC),
            P(SCEN, None, DEC),
            P(SCEN, DEC),
            P(None, SCEN, DEC),
        ),
        check_vma=False,
    )
```

```python
import jax
import jax.numpy as jnp
from jax import lax
from jax.experimental import pallas as pl
from jax.experimental.pallas import tpu as pltpu
from jax.sharding import Mesh
from jax.sharding import PartitionSpec as P

LEAF = 16
STEP = 0.5
F32 = jnp.float32
BF16 = jnp.bfloat16
VMEM_LIMIT = 48 * 1024 * 1024

NY, NQ, NR, NX = 4, 2, 4, 4
NZ = NQ * NR
SCEN = ("y", "zq", "zr", "x")
DEC = ("zh", "c")
EXTRA = 48
ARRIVED = (0, 4, 2, 6, 1, 5, 3, 7)


def exchange(value, axes):
    return lax.all_to_all(value, axes, 0, 0, tiled=True)


def spread(value, axes, count):
    return exchange(jnp.broadcast_to(value[None], (count,) + value.shape), axes)


def shift(value, axis, count, step):
    return lax.ppermute(value, axis, [((i + step) % count, i) for i in range(count)])


def flip(value, distance):
    return lax.ppermute(value, ("zq", "zr"), [(i, i ^ distance) for i in range(NZ)])


def split_two(value):
    high = value.astype(BF16)
    return high, (value - high.astype(F32)).astype(BF16)


def params(**more):
    return pltpu.CompilerParams(vmem_limit_bytes=VMEM_LIMIT, **more)


def cost(flops, size):
    return pl.CostEstimate(flops=flops, bytes_accessed=size, transcendentals=0)


def prepare_body(duals_ref, active_ref, weight_ref, recourse_ref, packed_ref, send_ref):
    rows, depth = duals_ref.shape
    tiles = active_ref.shape[0]
    width = depth // tiles
    blocks = rows // LEAF
    cols = send_ref.shape[2]
    weight = jnp.transpose(jnp.broadcast_to(weight_ref[...], (8, rows)))[:, :1]
    leaf_w = jnp.sum(weight.reshape(blocks, LEAF, 1), axis=1)
    own_w = jnp.sum(leaf_w, axis=0, keepdims=True)
    active = jnp.transpose(active_ref[...].astype(F32))
    highs, lows = [], []
    for tile in range(tiles):
        at = slice(tile * width, (tile + 1) * width)
        masked = duals_ref[:, at].astype(F32) * active[:, tile : tile + 1]
        packed_ref[EXTRA:, at] = masked.astype(BF16)
        leaf_v = jnp.sum((masked * weight).reshape(blocks, LEAF, width), axis=1)
        own_v = jnp.sum(leaf_v, axis=0, keepdims=True)
        high, low = split_two(own_v)
        highs.append(high.astype(F32))
        lows.append(low.astype(F32))
        high, low = split_two(leaf_v / leaf_w)
        packed_ref[:16, at] = high
        packed_ref[16:32, at] = low
        high, low = split_two(jnp.broadcast_to(own_v / own_w, (8, width)))
        packed_ref[32:48, at] = jnp.concatenate([high, low], 0)
    high, low = jnp.concatenate(highs, 1), jnp.concatenate(lows, 1)
    w_high, w_low = split_two(jnp.broadcast_to(own_w, (1, cols // 2)))
    tree = jnp.concatenate(
        [
            high[:, :cols],
            low[:, :cols],
            jnp.concatenate([high[:, cols:], low[:, cols:]], 1),
            jnp.concatenate([w_high.astype(F32), w_low.astype(F32)], 1),
        ],
        0,
    )
    for section in range(NX):
        send_ref[section] = jnp.concatenate([recourse_ref[section].astype(F32), tree], 0).astype(BF16)


def prepare(duals, active, weights, recourse):
    rows, depth = duals.shape
    sections, own_rows, cols = recourse.shape
    return pl.pallas_call(
        prepare_body,
        out_shape=(
            jax.ShapeDtypeStruct((rows + EXTRA, depth), BF16),
            jax.ShapeDtypeStruct((NX, own_rows + 4, cols), BF16),
        ),
        compiler_params=pltpu.CompilerParams(vmem_limit_bytes=60 * 1024 * 1024),
        cost_estimate=cost(4 * rows * depth, 4 * rows * depth),
    )(duals, active.T, weights[None], recourse)


def unpack_body(got_ref, slot_ref, tree_ref):
    own_rows = got_ref.shape[1] - 4
    cols = got_ref.shape[2]
    extra = tree_ref.shape[1] - cols - 128
    got = [got_ref[x].astype(F32) for x in range(NX)]
    slot_ref[...] = jnp.concatenate([part[:own_rows] for part in got], 0).astype(BF16)
    tree = sum(part[own_rows:] for part in got)
    tree_ref[:, :cols] = tree[0:1] + tree[1:2]
    tree_ref[:, cols : cols + extra] = tree[2:3, :extra] + tree[2:3, extra:]
    tree_ref[:, cols + extra :] = tree[3:4, :128] + tree[3:4, cols // 2 : cols // 2 + 128]


def unpack(got, depth):
    _, rows, cols = got.shape
    return pl.pallas_call(
        unpack_body,
        out_shape=(
            jax.ShapeDtypeStruct((NX * (rows - 4), cols), BF16),
            jax.ShapeDtypeStruct((1, depth + 128), F32),
        ),
        compiler_params=params(),
        cost_estimate=cost(1000, 1000000),
    )(got)


def products_body(x_ref, y_ref, z_ref, top_ref, left_ref, *refs):
    pieces, (nodes_ref, grads_ref, rhs_ref) = refs[:10], refs[10:]
    block = rhs_ref.shape[0] // (NY * NZ)

    def put(step, offset, value):
        place = lax.rem(y_ref[0] + step, NY) * NZ + (z_ref[0] ^ offset)
        rhs_ref[pl.ds(pl.multiple_of(place * block, block), block)] = value

    for part in range(2):
        here, up, down, over, under = pieces[5 * part : 5 * part + 5]
        for index, offset in enumerate(ARRIVED[4 * part : 4 * part + 4]):
            at = slice(index * block, (index + 1) * block)
            put(0, offset, here[at])
            put(1, offset, up[at])
            put(3, offset, down[at])
            put(2, offset, (over[at] if index < 2 else under[(index - 2) * block : (index - 1) * block]))
    rhs = rhs_ref[...]
    cols = rhs.shape[1]
    rows = left_ref.shape[0] // NX
    top = jnp.dot(top_ref[...], rhs, preferred_element_type=F32)
    middle = top[0:1] + top[1:2]
    base = top[2:3] + top[3:4]
    row = lax.broadcasted_iota(jnp.int32, (8, cols), 0)
    whole = jnp.dot(left_ref[...], rhs, preferred_element_type=F32)
    for to in range(NX):
        got = whole[to * rows : (to + 1) * rows]
        grads_ref[to] = got[EXTRA:].astype(BF16)
        step = lax.rem(to - x_ref[0] + NX, NX)
        nodes_ref[step, 0:16] = got[0:16] + got[16:32]
        mean = got[32:33] + got[40:41]
        nodes_ref[step, 16:24] = jnp.where(row == 0, mean, jnp.where(row == 1, middle, base))


def products(x_at, y_at, z_at, top, left, pieces):
    rows, depth = left.shape
    rows = rows // NX - EXTRA
    cols = pieces[0].shape[1]
    steps = 2
    wide = cols // steps
    whole = lambda value: pl.BlockSpec(value.shape, lambda j: (0, 0))
    return pl.pallas_call(
        products_body,
        grid=(steps,),
        in_specs=[pl.BlockSpec(memory_space=pltpu.SMEM)] * 3
        + [whole(top), whole(left)]
        + [pl.BlockSpec((value.shape[0], wide), lambda j: (0, j)) for value in pieces],
        out_specs=(
            pl.BlockSpec((NX, 24, wide), lambda j: (0, 0, j)),
            pl.BlockSpec((NX, rows, wide), lambda j: (0, 0, j)),
        ),
        out_shape=(
            jax.ShapeDtypeStruct((NX, 24, cols), F32),
            jax.ShapeDtypeStruct((NX, rows, cols), BF16),
        ),
        scratch_shapes=[pltpu.VMEM((depth, wide), BF16)],
        compiler_params=params(),
        cost_estimate=cost(2 * NX * (rows + EXTRA) * depth * cols, 10_000_000),
    )(x_at, y_at, z_at, top, left, *pieces)


def local(scen_duals, recourse, tile_active, scen_weights, cut_table, cut_count, center):
    rows, depth = scen_duals.shape
    sections, own_rows, cols = recourse.shape
    blocks = rows // LEAF
    x_at = lax.axis_index("x")[None]
    y_at = lax.axis_index("y")[None]
    z_at = lax.axis_index(("zq", "zr"))[None]
    together = lax.optimization_barrier

    packed, send = prepare(scen_duals, tile_active, scen_weights, recourse)
    own, tree = unpack(exchange(send, "x"), depth)
    own = own[None]
    left = lax.all_gather(packed, "x", axis=0, tiled=True)
    far = flip(own, 4)
    pair = jnp.concatenate([own, far], 0)
    four = jnp.concatenate([pair, flip(pair, 2)], 0)
    late = flip(four, 1)
    row = jnp.sum(spread(tree, "y", NY), axis=0)
    trees = spread(jnp.concatenate([tree, row], 0), ("zq", "zr"), NZ)

    four = four.reshape(-1, cols)
    late = late.reshape(-1, cols)
    half = four.shape[0] // 2
    four_up = shift(four, "y", NY, 1)
    four_down = shift(four, "y", NY, 3)
    late_up = shift(late, "y", NY, 1)
    late_down = shift(late, "y", NY, 3)
    four_over = shift(four_up[:half], "y", NY, 1)
    four_under = shift(four_down[half:], "y", NY, 3)
    late_over = shift(late_up[:half], "y", NY, 1)
    late_under = shift(late_down[half:], "y", NY, 3)
    pieces = (four, four_up, four_down, four_over, four_under)
    pieces += (late, late_up, late_down, late_over, late_under)

    trees = jnp.sum(trees.reshape(NQ, NR, 2, depth + 128), axis=1)
    middle = lax.dynamic_index_in_dim(trees[:, 0], lax.axis_index("zq"), 0)
    base = jnp.sum(trees[:, 1], axis=0, keepdims=True)
    upper = jnp.concatenate([middle, base], 0)
    upper = upper[:, :depth] / upper[:, depth : depth + 1]
    first = lax.reduce_precision(upper, 8, 7)
    second = (upper - first).astype(BF16)
    first = first.astype(BF16)
    top = jnp.concatenate([first[:1], second[:1], first[1:], second[1:], jnp.zeros((12, depth), BF16)], 0)

    nodes, grads = products(x_at, y_at, z_at, top, left, pieces)
    sent = [nodes[0]] + [shift(nodes[step], "x", NX, NX - step) for step in (1, 2, 3)]
    scen_subgrads = exchange(grads, "x")
    line = jnp.stack(sent)

    def of_section(section):
        return lax.dynamic_index_in_dim(line, lax.rem(x_at[0] - section + NX, NX), 0, keepdims=False)

    leaf_means = of_section(3)[:16]
    uppers = jnp.stack([of_section(0)[18], of_section(1)[17], of_section(2)[16]])
    node_means = jnp.concatenate(
        [jnp.broadcast_to(uppers[:, None, :], (3, blocks, cols)), leaf_means[None]], 0
    )
    new_cut = leaf_means.astype(BF16)
    slot_ids = jnp.arange(cut_table.shape[1], dtype=jnp.int32)
    slot_hit = slot_ids[None, :] == cut_count[:, None]
    new_cuts = jnp.where(slot_hit[:, :, None], new_cut[:, None, :], cut_table)
    active = slot_ids[None, :] <= cut_count[:, None]
    total = jnp.sum(jnp.where(active[:, :, None], new_cuts.astype(F32), 0.0), axis=1)
    aggregate = total / (cut_count.astype(F32) + 1.0)[:, None]
    squares = jnp.sum(aggregate * aggregate, axis=1)
    total_sq = lax.psum(squares, DEC)
    scale = jnp.sqrt(total_sq / (cols * 4) + 1e-05)
    new_center = center - STEP * aggregate / scale[:, None]
    return (node_means, new_cuts, new_center, scen_subgrads)


def solution(mesh):
    fine = Mesh(mesh.devices.reshape(NY, NQ, NR, NX, 2, 2), SCEN + DEC)
    placed = (
        P(SCEN, None),
        P(None, SCEN, DEC),
        P(SCEN, None),
        P(SCEN),
        P(SCEN, None, DEC),
        P(SCEN),
        P(SCEN, DEC),
    )
    return jax.shard_map(
        local,
        mesh=fine,
        in_specs=placed,
        out_specs=(
            P(None, SCEN, DEC),
            P(SCEN, None, DEC),
            P(SCEN, DEC),
            P(None, SCEN, DEC),
        ),
        check_vma=False,
    )
```

```python
import jax
import jax.numpy as jnp
from jax import lax
from jax.experimental import pallas as pl
from jax.experimental.pallas import tpu as pltpu
from jax.sharding import Mesh
from jax.sharding import PartitionSpec as P

LEAF = 16
STEP = 0.5
F32 = jnp.float32
BF16 = jnp.bfloat16
VMEM_LIMIT = 48 * 1024 * 1024

NY, NQ, NR, NX = 4, 2, 4, 4
NZ = NQ * NR
SCEN = ("y", "zq", "zr", "x")
DEC = ("zh", "c")
EXTRA = 48
ARRIVED = (0, 4, 2, 6, 1, 5, 3, 7)


def exchange(value, axes):
    return lax.all_to_all(value, axes, 0, 0, tiled=True)


def spread(value, axes, count):
    return exchange(jnp.broadcast_to(value[None], (count,) + value.shape), axes)


def shift(value, axis, count, step):
    return lax.ppermute(value, axis, [((i + step) % count, i) for i in range(count)])


def flip(value, distance):
    return lax.ppermute(value, ("zq", "zr"), [(i, i ^ distance) for i in range(NZ)])


def split_two(value):
    high = value.astype(BF16)
    return high, (value - high.astype(F32)).astype(BF16)


def params(**more):
    return pltpu.CompilerParams(vmem_limit_bytes=VMEM_LIMIT, **more)


def cost(flops, size):
    return pl.CostEstimate(flops=flops, bytes_accessed=size, transcendentals=0)


def prepare_body(duals_ref, active_ref, weight_ref, recourse_ref, packed_ref, send_ref):
    rows, depth = duals_ref.shape
    tiles = active_ref.shape[0]
    width = depth // tiles
    blocks = rows // LEAF
    cols = send_ref.shape[2]
    weight = jnp.transpose(jnp.broadcast_to(weight_ref[...], (8, rows)))[:, :1]
    leaf_w = jnp.sum(weight.reshape(blocks, LEAF, 1), axis=1)
    own_w = jnp.sum(leaf_w, axis=0, keepdims=True)
    active = jnp.transpose(active_ref[...].astype(F32))
    highs, lows = [], []
    for tile in range(tiles):
        at = slice(tile * width, (tile + 1) * width)
        masked = duals_ref[:, at].astype(F32) * active[:, tile : tile + 1]
        packed_ref[EXTRA:, at] = masked.astype(BF16)
        leaf_v = jnp.sum((masked * weight).reshape(blocks, LEAF, width), axis=1)
        own_v = jnp.sum(leaf_v, axis=0, keepdims=True)
        high, low = split_two(own_v)
        highs.append(high.astype(F32))
        lows.append(low.astype(F32))
        high, low = split_two(leaf_v / leaf_w)
        packed_ref[:16, at] = high
        packed_ref[16:32, at] = low
        high, low = split_two(jnp.broadcast_to(own_v / own_w, (8, width)))
        packed_ref[32:48, at] = jnp.concatenate([high, low], 0)
    high, low = jnp.concatenate(highs, 1), jnp.concatenate(lows, 1)
    w_high, w_low = split_two(jnp.broadcast_to(own_w, (1, cols // 2)))
    tree = jnp.concatenate(
        [
            high[:, :cols],
            low[:, :cols],
            jnp.concatenate([high[:, cols:], low[:, cols:]], 1),
            jnp.concatenate([w_high.astype(F32), w_low.astype(F32)], 1),
        ],
        0,
    )
    for section in range(NX):
        send_ref[section] = jnp.concatenate([recourse_ref[section].astype(F32), tree], 0).astype(BF16)


def prepare(duals, active, weights, recourse):
    rows, depth = duals.shape
    sections, own_rows, cols = recourse.shape
    return pl.pallas_call(
        prepare_body,
        out_shape=(
            jax.ShapeDtypeStruct((rows + EXTRA, depth), BF16),
            jax.ShapeDtypeStruct((NX, own_rows + 4, cols), BF16),
        ),
        compiler_params=pltpu.CompilerParams(vmem_limit_bytes=60 * 1024 * 1024),
        cost_estimate=cost(4 * rows * depth, 4 * rows * depth),
    )(duals, active.T, weights[None], recourse)


def unpack_body(got_ref, slot_ref, tree_ref):
    own_rows = got_ref.shape[1] - 4
    cols = got_ref.shape[2]
    extra = tree_ref.shape[1] - cols - 128
    got = [got_ref[x].astype(F32) for x in range(NX)]
    slot_ref[...] = jnp.concatenate([part[:own_rows] for part in got], 0).astype(BF16)
    tree = sum(part[own_rows:] for part in got)
    tree_ref[:, :cols] = tree[0:1] + tree[1:2]
    tree_ref[:, cols : cols + extra] = tree[2:3, :extra] + tree[2:3, extra:]
    tree_ref[:, cols + extra :] = tree[3:4, :128] + tree[3:4, cols // 2 : cols // 2 + 128]


def unpack(got, depth):
    _, rows, cols = got.shape
    return pl.pallas_call(
        unpack_body,
        out_shape=(
            jax.ShapeDtypeStruct((NX * (rows - 4), cols), BF16),
            jax.ShapeDtypeStruct((1, depth + 128), F32),
        ),
        compiler_params=params(),
        cost_estimate=cost(1000, 1000000),
    )(got)


def products_body(x_ref, y_ref, z_ref, top_ref, left_ref, *refs):
    pieces, (nodes_ref, grads_ref, rhs_ref) = refs[:10], refs[10:]
    block = rhs_ref.shape[0] // (NY * NZ)

    def put(step, offset, value):
        place = lax.rem(y_ref[0] + step, NY) * NZ + (z_ref[0] ^ offset)
        rhs_ref[pl.ds(pl.multiple_of(place * block, block), block)] = value

    for part in range(2):
        here, up, down, over, under = pieces[5 * part : 5 * part + 5]
        for index, offset in enumerate(ARRIVED[4 * part : 4 * part + 4]):
            at = slice(index * block, (index + 1) * block)
            put(0, offset, here[at])
            put(1, offset, up[at])
            put(3, offset, down[at])
            put(2, offset, (over[at] if index < 2 else under[(index - 2) * block : (index - 1) * block]))
    rhs = rhs_ref[...]
    cols = rhs.shape[1]
    rows = left_ref.shape[0] // NX
    top = jnp.dot(top_ref[...], rhs, preferred_element_type=F32)
    middle = top[0:1] + top[1:2]
    base = top[2:3] + top[3:4]
    row = lax.broadcasted_iota(jnp.int32, (8, cols), 0)
    whole = jnp.dot(left_ref[...], rhs, preferred_element_type=F32)
    for to in range(NX):
        got = whole[to * rows : (to + 1) * rows]
        grads_ref[to] = got[EXTRA:].astype(BF16)
        step = lax.rem(to - x_ref[0] + NX, NX)
        nodes_ref[step, 0:16] = got[0:16] + got[16:32]
        mean = got[32:33] + got[40:41]
        nodes_ref[step, 16:24] = jnp.where(row == 0, mean, jnp.where(row == 1, middle, base))


def products(x_at, y_at, z_at, top, left, pieces):
    rows, depth = left.shape
    rows = rows // NX - EXTRA
    cols = pieces[0].shape[1]
    steps = 2
    wide = cols // steps
    once = pl.Buffered(1)
    whole = lambda value: pl.BlockSpec(value.shape, lambda j: (0, 0), pipeline_mode=once)
    return pl.pallas_call(
        products_body,
        grid=(steps,),
        in_specs=[pl.BlockSpec(memory_space=pltpu.SMEM)] * 3
        + [whole(top), whole(left)]
        + [pl.BlockSpec((value.shape[0], wide), lambda j: (0, j)) for value in pieces],
        out_specs=(
            pl.BlockSpec((NX, 24, wide), lambda j: (0, 0, j)),
            pl.BlockSpec((NX, rows, wide), lambda j: (0, 0, j)),
        ),
        out_shape=(
            jax.ShapeDtypeStruct((NX, 24, cols), F32),
            jax.ShapeDtypeStruct((NX, rows, cols), BF16),
        ),
        scratch_shapes=[pltpu.VMEM((depth, wide), BF16)],
        compiler_params=pltpu.CompilerParams(vmem_limit_bytes=30 * 1024 * 1024),
        cost_estimate=cost(2 * NX * (rows + EXTRA) * depth * cols, 10_000_000),
    )(x_at, y_at, z_at, top, left, *pieces)


def local(scen_duals, recourse, tile_active, scen_weights, cut_table, cut_count, center):
    rows, depth = scen_duals.shape
    sections, own_rows, cols = recourse.shape
    blocks = rows // LEAF
    x_at = lax.axis_index("x")[None]
    y_at = lax.axis_index("y")[None]
    z_at = lax.axis_index(("zq", "zr"))[None]
    together = lax.optimization_barrier

    packed, send = prepare(scen_duals, tile_active, scen_weights, recourse)
    own, tree = unpack(exchange(send, "x"), depth)
    own = own[None]
    left = lax.all_gather(packed, "x", axis=0, tiled=True)
    far = flip(own, 4)
    pair = jnp.concatenate([own, far], 0)
    four = jnp.concatenate([pair, flip(pair, 2)], 0)
    late = flip(four, 1)
    row = jnp.sum(spread(tree, "y", NY), axis=0)
    trees = spread(jnp.concatenate([tree, row], 0), ("zq", "zr"), NZ)

    four = four.reshape(-1, cols)
    late = late.reshape(-1, cols)
    half = four.shape[0] // 2
    four_up = shift(four, "y", NY, 1)
    four_down = shift(four, "y", NY, 3)
    late_up = shift(late, "y", NY, 1)
    late_down = shift(late, "y", NY, 3)
    four_over = shift(four_up[:half], "y", NY, 1)
    four_under = shift(four_down[half:], "y", NY, 3)
    late_over = shift(late_up[:half], "y", NY, 1)
    late_under = shift(late_down[half:], "y", NY, 3)
    pieces = (four, four_up, four_down, four_over, four_under)
    pieces += (late, late_up, late_down, late_over, late_under)

    trees = jnp.sum(trees.reshape(NQ, NR, 2, depth + 128), axis=1)
    middle = lax.dynamic_index_in_dim(trees[:, 0], lax.axis_index("zq"), 0)
    base = jnp.sum(trees[:, 1], axis=0, keepdims=True)
    upper = jnp.concatenate([middle, base], 0)
    upper = upper[:, :depth] / upper[:, depth : depth + 1]
    first = lax.reduce_precision(upper, 8, 7)
    second = (upper - first).astype(BF16)
    first = first.astype(BF16)
    top = jnp.concatenate([first[:1], second[:1], first[1:], second[1:], jnp.zeros((12, depth), BF16)], 0)

    nodes, grads = products(x_at, y_at, z_at, top, left, pieces)
    sent = [nodes[0]] + [shift(nodes[step], "x", NX, NX - step) for step in (1, 2, 3)]
    scen_subgrads = exchange(grads, "x")
    line = jnp.stack(sent)

    def of_section(section):
        return lax.dynamic_index_in_dim(line, lax.rem(x_at[0] - section + NX, NX), 0, keepdims=False)

    leaf_means = of_section(3)[:16]
    uppers = jnp.stack([of_section(0)[18], of_section(1)[17], of_section(2)[16]])
    node_means = jnp.concatenate(
        [jnp.broadcast_to(uppers[:, None, :], (3, blocks, cols)), leaf_means[None]], 0
    )
    new_cut = leaf_means.astype(BF16)
    slot_ids = jnp.arange(cut_table.shape[1], dtype=jnp.int32)
    slot_hit = slot_ids[None, :] == cut_count[:, None]
    new_cuts = jnp.where(slot_hit[:, :, None], new_cut[:, None, :], cut_table)
    active = slot_ids[None, :] <= cut_count[:, None]
    total = jnp.sum(jnp.where(active[:, :, None], new_cuts.astype(F32), 0.0), axis=1)
    aggregate = total / (cut_count.astype(F32) + 1.0)[:, None]
    squares = jnp.sum(aggregate * aggregate, axis=1)
    total_sq = lax.psum(squares, DEC)
    scale = jnp.sqrt(total_sq / (cols * 4) + 1e-05)
    new_center = center - STEP * aggregate / scale[:, None]
    return (node_means, new_cuts, new_center, scen_subgrads)


def solution(mesh):
    fine = Mesh(mesh.devices.reshape(NY, NQ, NR, NX, 2, 2), SCEN + DEC)
    placed = (
        P(SCEN, None),
        P(None, SCEN, DEC),
        P(SCEN, None),
        P(SCEN),
        P(SCEN, None, DEC),
        P(SCEN),
        P(SCEN, DEC),
    )
    return jax.shard_map(
        local,
        mesh=fine,
        in_specs=placed,
        out_specs=(
            P(None, SCEN, DEC),
            P(SCEN, None, DEC),
            P(SCEN, DEC),
            P(None, SCEN, DEC),
        ),
        check_vma=False,
    )
```
